32 devices in a mesh: groups: 2 (over y), rows: 16 (over z, x, core).
Axes of the slice: x: 2, y: 2, z: 4, core: 2. Of those that a mesh axis runs over, the one named last changes fastest.
Arguments:
- snapshots: bfloat16 [32768, 4096], P(('groups', 'rows')), parts along dimension 0, may hold values from -100 to 100
- test_matrix: bfloat16 [4096, 80], replicated, may hold values from -6 to 6
Outputs:
- basis: float32 [32768, 80], P(('groups', 'rows')), parts along dimension 0
- coefficients: float32 [8192, 80], P(('groups', 'rows')), parts along dimension 0
The draws below stay inside these ranges and needn't reach their ends.
There are 2 independent parts, one for each index of `groups`. The reference program is written for one: setup_inputs(seed, part) draws one part's arguments, and reference() takes and returns one part's arrays. A program takes and returns all parts, laid end to end along the dimension named above; an argument that names none is the same for every part. Nothing has to cross between parts.
All inputs are finite; a program needn't handle non-finite values.
Results may differ from the reference program's by a relative error of at most 0.0039.
Values may be sent and summed in bfloat16 or wider, within the bound.
A program may use at most 64 MiB of HBM per device.

```python
import math
import jax
import jax.numpy as jnp
from jax import lax

SNAPS = 4096
SKETCH = 80
ROWS = 16384


def draw_snapshots(key, part):
    key = jax.random.fold_in(key, 11)
    subkeys = jax.random.split(key, 6)
    height = 1.0 + 2.0 * jnp.arange(ROWS, dtype=jnp.float32) / ROWS
    row_scale = height * jnp.exp(jax.random.uniform(subkeys[0], (ROWS,), jnp.float32, -0.7, 0.7))
    col_scale = jnp.exp(jax.random.uniform(subkeys[1], (SNAPS,), jnp.float32, -0.35, 0.35))
    mean_flow = 0.45 * jax.random.normal(subkeys[3], (ROWS, 1), jnp.float32)
    shapes = jax.random.normal(subkeys[4], (ROWS, 12), jnp.float32)
    weights = jax.random.normal(subkeys[5], (12, SNAPS), jnp.float32)
    turbulence = 0.3 * jax.random.normal(subkeys[2], (ROWS, SNAPS), jnp.float32)
    values = turbulence + mean_flow
    for number in range(12):
        amplitude = 0.25 * 0.8 ** number
        values = values + amplitude * shapes[:, number:number + 1] * weights[number:number + 1, :]
    values = values * row_scale[:, None] * col_scale[None, :]
    return values.astype(jnp.bfloat16)


def normal_values(key, dims, spread, bound, held_as=jnp.bfloat16):
    return jnp.clip(spread * jax.random.normal(key, dims, jnp.float32), -bound, bound).astype(held_as)


def setup_inputs(seed: int = 0, part: int = 0) -> dict:
    seeds = jax.random.split(jax.random.key(seed), 3)
    part_splits = jax.random.split(jax.random.fold_in(seeds[2], part), 3)
    return {
        "snapshots": draw_snapshots(jax.random.fold_in(jax.random.fold_in(seeds[2], part), 71), part),
        "test_matrix": normal_values(seeds[1], (SNAPS, SKETCH), 1.0, 6.0),
    }


def orthonormalize(sketch):
    gram_matrix = jnp.dot(sketch.T, sketch, precision=lax.Precision.HIGHEST)
    factor = jnp.linalg.cholesky(gram_matrix)
    return lax.linalg.triangular_solve(factor, sketch, left_side=False, lower=True, transpose_a=True)

def transpose_product(snapshots, half_basis):
    return lax.dot_general(snapshots.astype(jnp.float32), half_basis.astype(jnp.float32), (((0,), (0,)), ((), ())), preferred_element_type=jnp.float32)

def reference(snapshots, test_matrix):
    sketch = jnp.dot(snapshots.astype(jnp.float32), test_matrix.astype(jnp.float32), preferred_element_type=jnp.float32)
    first_basis = orthonormalize(sketch)
    first_half = first_basis.astype(jnp.bfloat16)
    projection = transpose_product(snapshots, first_half).astype(jnp.bfloat16)
    power = jnp.dot(snapshots.astype(jnp.float32), projection.astype(jnp.float32), preferred_element_type=jnp.float32)
    final_basis = orthonormalize(orthonormalize(power))
    final_half = final_basis.astype(jnp.bfloat16)
    coefficients = transpose_product(snapshots, final_half)
    basis = final_basis * math.sqrt(ROWS)
    return (basis, coefficients)
```

```python
import functools
import math

import jax
import jax.numpy as jnp
from jax import lax
from jax.experimental import pallas as pl
from jax.experimental.pallas import tpu as pltpu
from jax.sharding import PartitionSpec as P

MESH = pl.DeviceIdType.MESH
HIGHEST = lax.Precision.HIGHEST
BLOCK = 16
NT = (((1,), (1,)), ((), ()))
TN = (((0,), (0,)), ((), ()))


def row_digits(devices):
    digits, stride, chips = [(1, 2)], 2, devices // 2
    if (chips.bit_length() - 1) % 2:
        digits.append((stride, 2))
        stride, chips = stride * 2, chips // 2
    while chips > 1:
        digits.append((stride, 4))
        stride, chips = stride * 4, chips // 4
    return digits


def slot_of(index, digits, devices):
    slot, length = 0, devices
    for stride, size in digits:
        length //= size
        slot = slot + (index // stride) % size * length
    return slot


def inverse_factor(gram, work):
    size = gram.shape[0]
    work[pl.ds(0, size), :] = jnp.pad(gram, ((0, 0), (0, 128 - size)))
    lane = lax.broadcasted_iota(jnp.int32, (BLOCK, 128), 1)
    sub = lax.broadcasted_iota(jnp.int32, (BLOCK, 128), 0)

    def step(block, carry):
        start = pl.multiple_of(block * BLOCK, BLOCK)
        rows = work[pl.ds(start, BLOCK), :]
        rolled = pltpu.roll(rows, lax.rem(128 - start, 128), 1)
        columns = [jnp.broadcast_to(rolled[:, k:k + 1], (BLOCK, 128)) for k in range(BLOCK)]
        scale = jnp.zeros((BLOCK, 128), jnp.float32)
        for k in range(BLOCK):
            inverse = 1.0 / columns[k][k:k + 1, :]
            scale = jnp.where(sub == k, inverse, scale)
            below = sub > k
            times = jnp.where(below, columns[k] * inverse, 0.0)
            for l in range(k + 1, BLOCK):
                columns[l] = columns[l] - times * columns[l][k:k + 1, :]
            here = lane == start + k
            rows = jnp.where(here & below, 0.0, rows) - times * jnp.where(here[:1], 1.0, rows[k:k + 1, :])
            rolled = rolled - times * rolled[k:k + 1, :]
        diagonal = lane == start + sub
        unit = jnp.where(diagonal, 1.0, jnp.where((lane > start + sub) & (lane < start + BLOCK), 0.0, rows))
        update = lax.dot_general(
            rolled * scale, unit, TN, precision=HIGHEST, preferred_element_type=jnp.float32
        )
        rest = size - BLOCK
        later = pl.ds(pl.multiple_of(start + BLOCK, BLOCK), rest)
        wide = lax.broadcasted_iota(jnp.int32, (rest, 128), 1)
        old = work[later, :]
        work[later, :] = jnp.where((wide >= start) & (wide < start + BLOCK), 0.0, old) - update[BLOCK:size]
        lower = jnp.where(lane < start + sub, rows, jnp.where(diagonal, 1.0, 0.0))
        work[pl.ds(start, BLOCK), :] = lower * lax.rsqrt(1.0 / scale)
        return carry

    lax.fori_loop(0, size // BLOCK, step, 0)
    return work[pl.ds(0, size), :][:, :size]


def kernel(devices, groups_axis, rows_axis, a_hbm, tt_ref, basis_ref, coef_ref,
           a, yt, half, gram_own, gram_got, work, part, parts_got, gather, pt, cpart, cparts_got,
           a_sem, gram_sems, part_sems, gather_sems, cpart_sems):
    digits = row_digits(devices)
    me = lax.axis_index(rows_axis)
    total_rows = a.shape[0] * devices
    count, snaps = pt.shape
    rows = a.shape[0]
    width = snaps // devices
    tile = max(width, 256)
    blocks = a_sem.shape[0]
    step_rows = rows // blocks
    mine = [lax.rem(me // stride, size) for stride, size in digits]

    def peer(t, offset):
        stride, size = digits[t]
        return me + (lax.rem(mine[t] + offset, size) - mine[t]) * stride

    def copy_in(i):
        span = pl.ds(pl.multiple_of(i * step_rows, step_rows), step_rows)
        return pltpu.make_async_copy(a_hbm.at[span, :], a.at[span, :], a_sem.at[i])

    for i in range(blocks):
        copy_in(i).start()
    barrier = pltpu.get_barrier_semaphore()
    peers = 0
    for t, (stride, size) in enumerate(digits):
        for offset in range(1, size):
            pl.semaphore_signal(barrier, inc=1, device_id={rows_axis: peer(t, offset)}, device_id_type=MESH)
            peers += 1

    def send(src, dst, sems, t, offset):
        return pltpu.make_async_remote_copy(
            src_ref=src, dst_ref=dst, send_sem=sems.at[0, t, offset], recv_sem=sems.at[1, t, offset],
            device_id={rows_axis: peer(t, offset)}, device_id_type=MESH,
        )

    def gram_start(phase, t):
        copies = []
        for offset in range(1, digits[t][1]):
            copy = send(gram_own.at[phase, t], gram_got.at[phase, t, mine[t]], gram_sems.at[phase], t, offset)
            copy.start()
            copies.append(copy)
        return copies

    def gram_finish(phase, t, copies):
        for copy in copies:
            copy.wait()
        own = gram_own[phase, t]
        total = None
        for p in range(digits[t][1]):
            term = jnp.where(mine[t] == p, own, gram_got[phase, t, p])
            total = term if total is None else total + term
        if t + 1 < len(digits):
            gram_own[phase, t + 1] = total
        return total

    def local_gram(phase, matrix):
        gram_own[phase, 0] = lax.dot_general(
            matrix, matrix, NT, precision=HIGHEST, preferred_element_type=jnp.float32
        )

    def forward(i, left):
        span = pl.ds(pl.multiple_of(i * step_rows, step_rows), step_rows)
        yt[:, span] = lax.dot_general(left[...], a[span, :], NT, preferred_element_type=jnp.float32)

    def backward(target):
        def step(i, carry):
            start = pl.multiple_of(i * tile, tile)
            out = jnp.dot(half[...], a[:, pl.ds(start, tile)], preferred_element_type=jnp.float32)
            for j in range(tile // width):
                slot = slot_of(i * (tile // width) + j, digits, devices)
                target[slot] = out[:, j * width:(j + 1) * width].astype(target.dtype)
            return carry
        lax.fori_loop(0, snaps // tile, step, 0)

    def scatter_start(t, base, length, buffer, got, sems):
        copies = []
        for offset in range(1, digits[t][1]):
            p = lax.rem(mine[t] + offset, digits[t][1])
            copy = send(buffer.at[pl.ds(base + p * length, length)], got[t].at[mine[t]], sems, t, offset)
            copy.start()
            copies.append(copy)
        return copies

    def scatter_finish(t, base, length, buffer, got, copies):
        for copy in copies:
            copy.wait()
        size = digits[t][1]
        base = base + mine[t] * length

        def add(s, carry):
            total = buffer[base + s].astype(jnp.float32)
            for offset in range(1, size):
                total += got[t][lax.rem(mine[t] + offset, size), s].astype(jnp.float32)
            buffer[base + s] = total.astype(buffer.dtype)
            return carry
        lax.fori_loop(0, length, add, 0)
        return base

    def sketch(i, carry):
        copy_in(i).wait()
        forward(i, tt_ref)
        return carry

    lax.fori_loop(0, blocks, sketch, 0)
    local_gram(0, yt[...])
    pl.semaphore_wait(barrier, peers)
    for t in range(len(digits)):
        gram = gram_finish(0, t, gram_start(0, t))
    inverse = inverse_factor(gram, work)
    half[...] = jnp.dot(inverse, yt[...], precision=HIGHEST, preferred_element_type=jnp.float32).astype(half.dtype)

    backward(part)
    base, length, bases = 0, devices, []
    for t, (stride, size) in enumerate(digits):
        length //= size
        bases.append(base)
        base = scatter_finish(t, base, length, part, parts_got,
                              scatter_start(t, base, length, part, parts_got, part_sems))
    gather[base] = part[base].astype(gather.dtype)
    length = 1
    for t in reversed(range(len(digits))):
        copies = []
        for offset in range(1, digits[t][1]):
            span = gather.at[pl.ds(base, length)]
            copy = send(span, span, gather_sems, t, offset)
            copy.start()
            copies.append(copy)
        for copy in copies:
            copy.wait()
        base = bases[t]
        length *= digits[t][1]
    for d in range(devices):
        pt[:, d * width:(d + 1) * width] = gather[slot_of(d, digits, devices)]

    def power(i, carry):
        forward(i, pt)
        return carry

    lax.fori_loop(0, blocks, power, 0)
    local_gram(1, yt[...])
    for t in range(len(digits)):
        gram = gram_finish(1, t, gram_start(1, t))
    inverse = inverse_factor(gram, work)
    first = jnp.dot(inverse, yt[...], precision=HIGHEST, preferred_element_type=jnp.float32)
    yt[...] = first
    half[...] = first.astype(half.dtype)
    local_gram(2, first)
    gram_copies = gram_start(2, 0)
    backward(cpart)
    base, length = 0, devices
    for t, (stride, size) in enumerate(digits):
        length //= size
        copies = scatter_start(t, base, length, cpart, cparts_got, cpart_sems)
        gram = gram_finish(2, t, gram_copies)
        if t + 1 < len(digits):
            gram_copies = gram_start(2, t + 1)
        else:
            inverse = inverse_factor(gram, work)
            last = jnp.dot(inverse, yt[...], precision=HIGHEST, preferred_element_type=jnp.float32)
            basis_ref[...] = (last * math.sqrt(total_rows)).T
        base = scatter_finish(t, base, length, cpart, cparts_got, copies)
    coef = jnp.dot(inverse, cpart[base].astype(jnp.float32), precision=HIGHEST, preferred_element_type=jnp.float32)
    coef_ref[...] = coef.T


def shards(snapshots, test_matrix):
    devices = lax.axis_size("rows")
    rows, snaps = snapshots.shape
    count = test_matrix.shape[1]
    digits = row_digits(devices)
    width = snaps // devices
    stages = len(digits)
    widest = max(size for _, size in digits)
    blocks = 8
    got, length = [], devices
    for _, size in digits:
        length //= size
        got.append((size, length, count, width))
    f32, bf16 = jnp.float32, jnp.bfloat16
    vmem = pl.BlockSpec(memory_space=pltpu.VMEM)
    return pl.pallas_call(
        functools.partial(kernel, devices, "groups", "rows"),
        out_shape=(
            jax.ShapeDtypeStruct((rows, count), f32),
            jax.ShapeDtypeStruct((width, count), f32),
        ),
        in_specs=[pl.BlockSpec(memory_space=pl.ANY), vmem],
        out_specs=(vmem, vmem),
        scratch_shapes=[
            pltpu.VMEM((rows, snaps), bf16),
            pltpu.VMEM((count, rows), f32),
            pltpu.VMEM((count, rows), bf16),
            pltpu.VMEM((3, stages, count, count), f32),
            pltpu.VMEM((3, stages, widest, count, count), f32),
            pltpu.VMEM((2 * count, 128), f32),
            pltpu.VMEM((devices, count, width), f32),
            [pltpu.VMEM(shape, f32) for shape in got],
            pltpu.VMEM((devices, count, width), bf16),
            pltpu.VMEM((count, snaps), bf16),
            pltpu.VMEM((devices, count, width), bf16),
            [pltpu.VMEM(shape, bf16) for shape in got],
            pltpu.SemaphoreType.DMA((blocks,)),
            pltpu.SemaphoreType.DMA((3, 2, stages, widest)),
            pltpu.SemaphoreType.DMA((2, stages, widest)),
            pltpu.SemaphoreType.DMA((2, stages, widest)),
            pltpu.SemaphoreType.DMA((2, stages, widest)),
        ],
        compiler_params=pltpu.CompilerParams(
            collective_id=0, has_side_effects=True, vmem_limit_bytes=56 * 2**20
        ),
    )(snapshots, test_matrix.T)


def solution(mesh):
    in_specs = (P(("groups", "rows"), None), P())
    out_specs = (P(("groups", "rows"), None), P(("groups", "rows"), None))
    return jax.shard_map(shards, mesh=mesh, in_specs=in_specs, out_specs=out_specs, check_vma=False)
```

```python
import functools
import itertools
import math

import jax
import jax.numpy as jnp
from jax import lax
from jax.experimental import pallas as pl
from jax.experimental.pallas import tpu as pltpu
from jax.sharding import PartitionSpec as P

MESH = pl.DeviceIdType.MESH
HIGHEST = lax.Precision.HIGHEST
BLOCK = 16
NT = (((1,), (1,)), ((), ()))
TN = (((0,), (0,)), ((), ()))


def row_digits(devices):
    digits, stride, chips = [(1, 2)], 2, devices // 2
    if (chips.bit_length() - 1) % 2:
        digits.append((stride, 2))
        stride, chips = stride * 2, chips // 2
    while chips > 1:
        digits.append((stride, 4))
        stride, chips = stride * 4, chips // 4
    return digits


def offsets_of(digits):
    offsets = list(itertools.product(*[range(size) for _, size in digits]))
    return sorted(offsets, key=lambda o: [o[t] == 0 for t in range(len(o))])


def number_of(offset, digits, first=0):
    number = 0
    for t in range(first, len(digits)):
        number = number * digits[t][1] + offset[t]
    return number


def split_of(size):
    return -(-size // (2 * BLOCK)) * BLOCK


def packed(gram):
    size = gram.shape[0]
    split = split_of(size)
    wide = jnp.pad(gram, ((0, 0), (0, 128 - size)))
    beside = jnp.pad(pltpu.roll(wide[split:], size - split, 1), ((0, 2 * split - size), (0, 0)))
    lane = lax.broadcasted_iota(jnp.int32, (split, 128), 1)
    return jnp.where(lane < size, wide[:split], jnp.where(lane < 2 * size - split, beside, 0.0))


def inverse_factor(gram, work, size):
    split, rest = gram.shape[0], size - gram.shape[0]
    work[pl.ds(0, split), :] = gram
    work[pl.ds(split, rest), :] = pltpu.roll(gram[:rest], 128 - (size - split), 1)
    lane = lax.broadcasted_iota(jnp.int32, (BLOCK, 128), 1)
    sub = lax.broadcasted_iota(jnp.int32, (BLOCK, 128), 0)

    def step(block, carry):
        start = pl.multiple_of(block * BLOCK, BLOCK)
        rows = work[pl.ds(start, BLOCK), :]
        rolled = pltpu.roll(rows, lax.rem(128 - start, 128), 1)
        columns = [jnp.broadcast_to(rolled[:, k:k + 1], (BLOCK, 128)) for k in range(BLOCK)]
        scale = jnp.zeros((BLOCK, 128), jnp.float32)
        for k in range(BLOCK):
            inverse = 1.0 / columns[k][k:k + 1, :]
            scale = jnp.where(sub == k, inverse, scale)
            below = sub > k
            times = jnp.where(below, columns[k] * inverse, 0.0)
            for l in range(k + 1, BLOCK):
                columns[l] = columns[l] - times * columns[l][k:k + 1, :]
            here = lane == start + k
            rows = jnp.where(here & below, 0.0, rows) - times * jnp.where(here[:1], 1.0, rows[k:k + 1, :])
            rolled = rolled - times * rolled[k:k + 1, :]
        diagonal = lane == start + sub
        unit = jnp.where(diagonal, 1.0, jnp.where((lane > start + sub) & (lane < start + BLOCK), 0.0, rows))
        update = lax.dot_general(
            rolled * scale, unit, TN, precision=HIGHEST, preferred_element_type=jnp.float32
        )
        rest = size - BLOCK
        later = pl.ds(pl.multiple_of(start + BLOCK, BLOCK), rest)
        wide = lax.broadcasted_iota(jnp.int32, (rest, 128), 1)
        old = work[later, :]
        work[later, :] = jnp.where((wide >= start) & (wide < start + BLOCK), 0.0, old) - update[BLOCK:size]
        lower = jnp.where(lane < start + sub, rows, jnp.where(diagonal, 1.0, 0.0))
        work[pl.ds(start, BLOCK), :] = lower * lax.rsqrt(1.0 / scale)
        return carry

    lax.fori_loop(0, size // BLOCK, step, 0)
    return work[pl.ds(0, size), :][:, :size]


def kernel(devices, groups_axis, rows_axis, a_hbm, tt_ref, basis_ref, coef_ref,
           a, yt, half, gram_own, gram_got, work, part, parts_got, gather, pt, cpart, cparts_got,
           a_sem, gram_sems, part_sems, gather_sems, cpart_sems):
    digits = row_digits(devices)
    me = lax.axis_index(rows_axis)
    total_rows = a.shape[0] * devices
    count, snaps = pt.shape
    rows = a.shape[0]
    width = snaps // devices
    tile = max(width, 256)
    blocks = a_sem.shape[0]
    step_rows = rows // blocks
    mine = [lax.rem(me // stride, size) for stride, size in digits]

    def peer(t, offset):
        stride, size = digits[t]
        return me + (lax.rem(mine[t] + offset, size) - mine[t]) * stride

    def copy_in(i):
        span = pl.ds(pl.multiple_of(i * step_rows, step_rows), step_rows)
        return pltpu.make_async_copy(a_hbm.at[span, :], a.at[span, :], a_sem.at[i])

    for i in range(blocks):
        copy_in(i).start()
    barrier = pltpu.get_barrier_semaphore()
    peers = 0
    for t, (stride, size) in enumerate(digits):
        for offset in range(1, size):
            pl.semaphore_signal(barrier, inc=1, device_id={rows_axis: peer(t, offset)}, device_id_type=MESH)
            peers += 1

    def send(src, dst, sems, t, offset):
        return pltpu.make_async_remote_copy(
            src_ref=src, dst_ref=dst, send_sem=sems.at[0, t, offset], recv_sem=sems.at[1, t, offset],
            device_id={rows_axis: peer(t, offset)}, device_id_type=MESH,
        )

    def gram_start(phase, t):
        copies = []
        for offset in range(1, digits[t][1]):
            copy = send(gram_own.at[phase, t], gram_got.at[phase, t, mine[t]], gram_sems.at[phase], t, offset)
            copy.start()
            copies.append(copy)
        return copies

    def gram_finish(phase, t, copies):
        for copy in copies:
            copy.wait()
        own = gram_own[phase, t]
        total = None
        for p in range(digits[t][1]):
            term = jnp.where(mine[t] == p, own, gram_got[phase, t, p])
            total = term if total is None else total + term
        if t + 1 < len(digits):
            gram_own[phase, t + 1] = total
        return total

    def local_gram(phase, matrix):
        gram_own[phase, 0] = packed(lax.dot_general(
            matrix, matrix, NT, precision=HIGHEST, preferred_element_type=jnp.float32
        ))

    def forward(i, left):
        span = pl.ds(pl.multiple_of(i * step_rows, step_rows), step_rows)
        yt[:, span] = lax.dot_general(left[...], a[span, :], NT, preferred_element_type=jnp.float32)

    def moved(offset, sign):
        place = me
        for t, (stride, size) in enumerate(digits):
            if offset[t]:
                place = place + (lax.rem(mine[t] + sign * offset[t] + size, size) - mine[t]) * stride
        return place

    def change(offset, t, value):
        return offset[:t] + (value,) + offset[t + 1:]

    aligned = width % 128 == 0

    def columns_of(place):
        return pl.ds(pl.multiple_of(place * width, width), width)

    def scatter(buffer, got, sems):
        copies = {}

        def compute(offset):
            if aligned:
                place = moved(offset, 1)
                out = jnp.dot(half[...], a[:, columns_of(place)], preferred_element_type=jnp.float32)
                buffer[place] = out.astype(buffer.dtype)

        def put(t, offset):
            copies[offset] = copy = pltpu.make_async_remote_copy(
                src_ref=buffer.at[moved(offset, 1)],
                dst_ref=got[t].at[offset[t] - 1, number_of(offset, digits, t + 1)],
                send_sem=sems.at[0, number_of(offset, digits)], recv_sem=sems.at[1, number_of(offset, digits)],
                device_id={rows_axis: peer(t, offset[t])}, device_id_type=MESH,
            )
            copy.start()

        def take(t, offset):
            place = moved(offset, 1)
            total = buffer[place].astype(jnp.float32)
            for p in range(1, digits[t][1]):
                copies[change(offset, t, p)].wait_recv()
                total += got[t][p - 1, number_of(offset, digits, t + 1)].astype(jnp.float32)
            buffer[place] = total.astype(buffer.dtype)
            if t + 1 < len(digits) and offset[t + 1]:
                put(t + 1, offset)

        if not aligned:
            def step(i, carry):
                start = pl.multiple_of(i * tile, tile)
                out = jnp.dot(half[...], a[:, pl.ds(start, tile)], preferred_element_type=jnp.float32)
                for j in range(tile // width):
                    buffer[i * (tile // width) + j] = out[:, j * width:(j + 1) * width].astype(buffer.dtype)
                return carry
            lax.fori_loop(0, snaps // tile, step, 0)
        held = [o for o in offsets_of(digits) if o[0] == 0]
        for i, offset in enumerate(held):
            for p in range(1, digits[0][1]):
                compute(change(offset, 0, p))
                put(0, change(offset, 0, p))
            compute(offset)
            if i >= 2:
                take(0, held[i - 2])
            yield
        for offset in held[-2:]:
            take(0, offset)
            yield
        for t in range(1, len(digits)):
            for offset in held:
                if not any(offset[:t + 1]):
                    take(t, offset)
                    yield
        for copy in copies.values():
            copy.wait_send()

    def spread(use):
        copies = {}

        def forward_to(t, offset):
            block = gather.at[moved(offset, -1)]
            for p in range(1, digits[t][1]):
                there = change(offset, t, p)
                number = number_of(there, digits)
                copies[there] = copy = pltpu.make_async_remote_copy(
                    src_ref=block, dst_ref=block, send_sem=gather_sems.at[0, number],
                    recv_sem=gather_sems.at[1, number],
                    device_id={rows_axis: peer(t, p)}, device_id_type=MESH,
                )
                copy.start()

        def arrived(last, offset):
            for t in reversed(range(last)):
                forward_to(t, offset)
            use(moved(offset, -1), not any(offset))

        arrived(len(digits), (0,) * len(digits))
        for t in reversed(range(len(digits))):
            for offset in reversed(offsets_of(digits)):
                if offset[t] and not any(offset[:t]):
                    copies[offset].wait_recv()
                    arrived(t, offset)
        for copy in copies.values():
            copy.wait_send()

    def sketch(i, carry):
        copy_in(i).wait()
        forward(i, tt_ref)
        return carry

    lax.fori_loop(0, blocks, sketch, 0)
    local_gram(0, yt[...])
    pl.semaphore_wait(barrier, peers)
    for t in range(len(digits)):
        gram = gram_finish(0, t, gram_start(0, t))
    inverse = inverse_factor(gram, work, count)
    half[...] = jnp.dot(inverse, yt[...], precision=HIGHEST, preferred_element_type=jnp.float32).astype(half.dtype)

    for _ in scatter(part, parts_got, part_sems):
        pass
    gather[me] = part[me].astype(gather.dtype)

    def power(place, is_first):
        if aligned:
            term = lax.dot_general(gather[place], a[:, columns_of(place)], NT, preferred_element_type=jnp.float32)
            yt[...] = term if is_first else yt[...] + term

    spread(power)
    if not aligned:
        for d in range(devices):
            pt[:, d * width:(d + 1) * width] = gather[d]

        def power_rows(i, carry):
            forward(i, pt)
            return carry

        lax.fori_loop(0, blocks, power_rows, 0)
    local_gram(1, yt[...])
    for t in range(len(digits)):
        gram = gram_finish(1, t, gram_start(1, t))
    inverse = inverse_factor(gram, work, count)
    first = jnp.dot(inverse, yt[...], precision=HIGHEST, preferred_element_type=jnp.float32)
    yt[...] = first
    half[...] = first.astype(half.dtype)
    local_gram(2, first)
    steps = scatter(cpart, cparts_got, cpart_sems)
    held = devices // digits[0][1]
    for t in range(len(digits)):
        gram_copies = gram_start(2, t)
        for _ in range(held // len(digits) + 1):
            next(steps, None)
        gram = gram_finish(2, t, gram_copies)
    inverse = inverse_factor(gram, work, count)
    last = jnp.dot(inverse, yt[...], precision=HIGHEST, preferred_element_type=jnp.float32)
    basis_ref[...] = last * math.sqrt(total_rows)
    for _ in steps:
        pass
    coef_ref[...] = jnp.dot(
        inverse, cpart[me].astype(jnp.float32), precision=HIGHEST, preferred_element_type=jnp.float32
    )


def shards(snapshots, test_matrix):
    devices = lax.axis_size("rows")
    rows, snaps = snapshots.shape
    count = test_matrix.shape[1]
    digits = row_digits(devices)
    width = snaps // devices
    stages = len(digits)
    widest = max(size for _, size in digits)
    blocks = 8
    got, length = [], devices
    for _, size in digits:
        length //= size
        got.append((size - 1, length, count, width))
    f32, bf16 = jnp.float32, jnp.bfloat16
    vmem = pl.BlockSpec(memory_space=pltpu.VMEM)
    basis, coefficients = pl.pallas_call(
        functools.partial(kernel, devices, "groups", "rows"),
        out_shape=(
            jax.ShapeDtypeStruct((count, rows), f32),
            jax.ShapeDtypeStruct((count, width), f32),
        ),
        in_specs=[pl.BlockSpec(memory_space=pl.ANY), vmem],
        out_specs=(vmem, vmem),
        scratch_shapes=[
            pltpu.VMEM((rows, snaps), bf16),
            pltpu.VMEM((count, rows), f32),
            pltpu.VMEM((count, rows), bf16),
            pltpu.VMEM((3, stages, split_of(count), 128), f32),
            pltpu.VMEM((3, stages, widest, split_of(count), 128), f32),
            pltpu.VMEM((2 * count, 128), f32),
            pltpu.VMEM((devices, count, width), f32),
            [pltpu.VMEM(shape, f32) for shape in got],
            pltpu.VMEM((devices, count, width), bf16),
            pltpu.VMEM((count, snaps), bf16),
            pltpu.VMEM((devices, count, width), bf16),
            [pltpu.VMEM(shape, bf16) for shape in got],
            pltpu.SemaphoreType.DMA((blocks,)),
            pltpu.SemaphoreType.DMA((3, 2, stages, widest)),
            pltpu.SemaphoreType.DMA((2, devices)),
            pltpu.SemaphoreType.DMA((2, devices)),
            pltpu.SemaphoreType.DMA((2, devices)),
        ],
        compiler_params=pltpu.CompilerParams(
            collective_id=0, has_side_effects=True, vmem_limit_bytes=56 * 2**20
        ),
    )(snapshots, test_matrix.T)
    return basis.T, coefficients.T


def solution(mesh):
    in_specs = (P(("groups", "rows"), None), P())
    out_specs = (P(("groups", "rows"), None), P(("groups", "rows"), None))
    return jax.shard_map(shards, mesh=mesh, in_specs=in_specs, out_specs=out_specs, check_vma=False)
```
